32 devices in a mesh: groups: 2 (over y), tile: 4 (over z), dp: 2 (over x), chan: 2 (over core).
Axes of the slice: x: 2, y: 2, z: 4, core: 2. Of those that a mesh axis runs over, the one named last changes fastest.
Arguments:
- activations: bfloat16 [8, 64, 32, 256], P(('groups', 'dp'), 'chan', 'tile'), parts along dimension 0, may hold values from -6 to 6
- occupancy: int32 [8, 4, 2, 2], P(('groups', 'dp'), 'tile'), parts along dimension 0, may hold values 0 or 1
- weight: bfloat16 [27, 64, 64], replicated, may hold values from -0.15625 to 0.15625
- cotangent: bfloat16 [8, 64, 32, 256], P(('groups', 'dp'), 'chan', 'tile'), parts along dimension 0, may hold values from -6 to 6
Outputs:
- output: bfloat16 [8, 64, 32, 256], P(('groups', 'dp'), 'chan', 'tile'), parts along dimension 0
- input_grad: bfloat16 [8, 64, 32, 256], P(('groups', 'dp'), 'chan', 'tile'), parts along dimension 0
- weight_grad: float32 [54, 64, 64], P('groups', 'chan'), parts along dimension 0
The draws below stay inside these ranges and needn't reach their ends.
There are 2 independent parts, one for each index of `groups`. The reference program is written for one: setup_inputs(seed, part) draws one part's arguments, and reference() takes and returns one part's arrays. A program takes and returns all parts, laid end to end along the dimension named above; an argument that names none is the same for every part. Nothing has to cross between parts.
Inputs may be any that keep to these rules, and one draw needn't show every extreme that they name: `occupancy`: 1 marks a tile that holds tissue, 0 an empty one.
All inputs are finite; a program needn't handle non-finite values. No bound on the sum of `occupancy` on one device may be relied on, other than what follows from the above.
Results may differ from the reference program's by a relative error of at most 0.003.
Values may be sent and summed in bfloat16 or wider, within the bound.
A program may use at most 64 MiB of HBM per device.

```python
import jax
import jax.numpy as jnp

C = 64
E = 8
GX = 2
GY = 2
BATCH = 4
LAYERS = 4
ZDIM = 32
PLANE = 256


def place_ends(entries, stream_key, smallest, largest):
    place = [jax.random.randint(jax.random.fold_in(stream_key, axis), (), 0, length) for axis, length in enumerate(entries.shape)]
    widest = entries.shape.index(max(entries.shape))
    neighbour = place[:widest] + [(place[widest] + 1) % entries.shape[widest]] + place[widest + 1:]
    return entries.at[tuple(place)].set(smallest).at[tuple(neighbour)].set(largest)


def steps_of(key, dims, split, smallest, top_value):
    def one(dim, blocks):
        heights = jax.random.uniform(jax.random.fold_in(jax.random.fold_in(key, 6), dim), (blocks,), jnp.float32, smallest / len(split), top_value / len(split))
        return jnp.repeat(jnp.exp(heights), dims[dim] // blocks).reshape((-1,) + (1,) * (len(dims) - dim - 1))

    loudness = one(*split[0])
    for cut in split[1:]:
        loudness = loudness * one(*cut)
    return loudness


def noise(own_key, dims, scale, reach, split=(), kind=jnp.bfloat16):
    array = scale * jax.random.normal(own_key, dims, jnp.float32)
    if split:
        array = array * steps_of(own_key, dims, split, -0.22, 0.18)
    return jnp.clip(array, -reach, reach).astype(kind)


def setup_inputs(seed: int = 0, part: int = 0) -> dict:
    key_of = jax.random.split(jax.random.key(seed), 5)
    own_keys = jax.random.split(jax.random.fold_in(key_of[4], part), 5)
    activations = noise(own_keys[0], (BATCH, C, ZDIM, PLANE), 1.0, 6.0, ((0, 2), (1, 2), (2, 4)))
    occupancy = place_ends((jax.random.randint(own_keys[1], (BATCH, LAYERS, GX, GY), 0, 4) < 3).astype(jnp.int32), jax.random.fold_in(own_keys[1], 1), 0, 1)
    weight = noise(key_of[2], (27, C, C), (27 * C) ** -0.5, 0.15625)
    cotangent = noise(own_keys[3], (BATCH, C, ZDIM, PLANE), 1.0, 6.0, ((0, 2), (1, 2), (2, 4)))
    return dict(activations=activations, occupancy=occupancy, weight=weight, cotangent=cotangent)


def voxel_live(occupancy):
    batches, layers, tiles_x, tiles_y = occupancy.shape
    spread = jnp.broadcast_to(occupancy[:, :, None, :, None, :, None], (batches, layers, E, tiles_x, E, tiles_y, E))
    return spread.reshape(batches, 1, layers * E, tiles_x * E * tiles_y * E)

def pad_volume(field):
    batches, channels, depth, plane_size = field.shape
    shaped = field.astype(jnp.float32).reshape(batches, channels, depth, GX * E, GY * E)
    return jnp.pad(shaped, ((0, 0), (0, 0), (1, 1), (1, 1), (1, 1)))

def window(padded, along_z, along_x, along_y):
    batches, channels, depth, width_x, width_y = padded.shape
    part = padded[:, :, along_z:along_z + depth - 2, along_x:along_x + width_x - 2, along_y:along_y + width_y - 2]
    return part.reshape(batches, channels, (depth - 2) * (width_x - 2) * (width_y - 2))

def offsets():
    return [(along_z, along_x, along_y) for along_z in range(3) for along_x in range(3) for along_y in range(3)]

def reference(activations, occupancy, weight, cotangent):
    live_mask = voxel_live(occupancy).astype(jnp.bfloat16)
    masked = activations * live_mask
    live_wide = live_mask.astype(jnp.float32)
    weight_wide = weight.astype(jnp.float32)
    shape_flat = (activations.shape[0], activations.shape[1], activations.shape[2] * activations.shape[3])
    masked_pad = pad_volume(masked)
    summed = jnp.zeros(shape_flat, jnp.float32)
    for position, (along_z, along_x, along_y) in enumerate(offsets()):
        summed = summed + jnp.einsum('oi,biv->bov', weight_wide[position], window(masked_pad, along_z, along_x, along_y))
    summed = summed.reshape(activations.shape)
    logistic = jax.nn.sigmoid(summed)
    output = (live_wide * (masked.astype(jnp.float32) + summed * logistic)).astype(jnp.bfloat16)
    slope = logistic * (1.0 + summed * (1.0 - logistic))
    grad_pre = (cotangent.astype(jnp.float32) * live_wide * slope).astype(jnp.bfloat16)
    grad_pad = pad_volume(grad_pre)
    back = jnp.zeros(shape_flat, jnp.float32)
    for position, (along_z, along_x, along_y) in enumerate(offsets()):
        back = back + jnp.einsum('oi,bov->biv', weight_wide[position], window(grad_pad, 2 - along_z, 2 - along_x, 2 - along_y))
    back = back.reshape(activations.shape)
    input_grad = (live_wide * (cotangent.astype(jnp.float32) + back)).astype(jnp.bfloat16)
    grad_wide = grad_pre.astype(jnp.float32).reshape(shape_flat)
    pieces = []
    for position, (along_z, along_x, along_y) in enumerate(offsets()):
        pieces.append(jnp.einsum('bov,biv->oi', grad_wide, window(masked_pad, along_z, along_x, along_y)))
    count = shape_flat[0] * shape_flat[2]
    weight_grad = jnp.stack(pieces) / jnp.sqrt(jnp.float32(count))
    return (output, input_grad, weight_grad)
```

```python
import functools
import math

import jax
import jax.numpy as jnp
from jax import lax
from jax.experimental import pallas as pl
from jax.experimental.pallas import tpu as pltpu
from jax.sharding import PartitionSpec as P

E = 8
GX = 2
GY = 2
WY = GY * E
PLANE = GX * E * WY
MESH = pl.DeviceIdType.MESH
BF16 = jnp.bfloat16
F32 = jnp.float32
ROWS = 16
TILES = 27


def dot(a, b):
    return lax.dot_general(a, b, (((1,), (0,)), ((), ())), preferred_element_type=F32)


def dot_nt(a, b):
    return lax.dot_general(a, b, (((1,), (1,)), ((), ())), preferred_element_type=F32)


def lanes(rows):
    return lax.broadcasted_iota(jnp.int32, (rows, PLANE), 1)


def kernel(
    tiles, dps, scale,
    act, cot, occ, w, out, grad_in, wg,
    x, xe, g, ge, gd, wf, wb, part, landed, total,
    xs, xr, gs, gr, rs, rr, ts, tr,
):
    batches, half, inner = act.shape
    depth = inner // PLANE
    me = {name: lax.axis_index(name) for name in ("tile", "dp", "chan")}
    t, c = me["tile"], me["chan"]
    other = 1 - c
    count = tiles * dps
    rank = t * dps + me["dp"]
    has_up = t < tiles - 1
    has_down = t > 0

    def member(j):
        r = lax.rem(rank + j, count)
        return r, {"tile": r // dps, "dp": lax.rem(r, dps)}

    barrier = pltpu.get_barrier_semaphore()

    def greet(device):
        pl.semaphore_signal(barrier, inc=1, device_id=device, device_id_type=MESH)

    greet({"chan": other})

    @pl.when(has_up)
    def _():
        greet({"tile": t + 1, "chan": other})

    @pl.when(has_down)
    def _():
        greet({"tile": t - 1, "chan": other})

    @pl.loop(1, count)
    def _(j):
        greet(member(j)[1])

    place = lanes(half)
    row = place // WY
    col = place % WY
    from_left = jnp.where(col > 0, 1.0, 0.0).astype(BF16)
    from_right = jnp.where(col < WY - 1, 1.0, 0.0).astype(BF16)
    has_above = row > 0
    has_below = row < GX * E - 1

    def live_of(b):
        def pick(i):
            return jnp.where(col < E, occ[b, 0, i, 0], occ[b, 0, i, 1])
        return jnp.where(row < E, pick(0), pick(1)).astype(F32)

    live = [live_of(b) for b in range(batches)]

    def spread(dst, b, q, ch, value, flip):
        first, last = (2, 0) if flip else (0, 2)
        dst[b, 3 * q + first, ch] = pltpu.roll(value, 1, 1) * from_left
        dst[b, 3 * q + 1, ch] = value
        dst[b, 3 * q + last, ch] = pltpu.roll(value, PLANE - 1, 1) * from_right

    def rim_zero(buf):
        zeros = jnp.zeros((half, PLANE), BF16)

        @pl.when(jnp.logical_not(has_down))
        def _():
            for b in range(batches):
                for ch in range(2):
                    buf[b, 0, ch] = zeros

        @pl.when(jnp.logical_not(has_up))
        def _():
            for b in range(batches):
                for ch in range(2):
                    buf[b, depth + 1, ch] = zeros

    def inside(buf, b, ch, send, recv):
        ref = buf.at[b, pl.ds(1, depth), ch]
        return pltpu.make_async_remote_copy(
            src_ref=ref, dst_ref=ref, send_sem=send.at[b, 0], recv_sem=recv.at[b, 0],
            device_id={"chan": other}, device_id_type=MESH,
        )

    def rim(buf, b, ch, up, to, send, recv):
        side = 1 if up else 3
        return pltpu.make_async_remote_copy(
            src_ref=buf.at[b, depth if up else 1, ch],
            dst_ref=buf.at[b, 0 if up else depth + 1, ch],
            send_sem=send.at[b, side + to], recv_sem=recv.at[b, side + ch],
            device_id={"tile": t + 1 if up else t - 1, "chan": to}, device_id_type=MESH,
        )

    def send_all(buf, b, send, recv):
        @pl.when(has_up)
        def _():
            for to in range(2):
                rim(buf, b, c, True, to, send, recv).start()

        @pl.when(has_down)
        def _():
            for to in range(2):
                rim(buf, b, c, False, to, send, recv).start()

        inside(buf, b, c, send, recv).start()

    def sent_all(buf, b, send, recv):
        @pl.when(has_up)
        def _():
            for to in range(2):
                rim(buf, b, c, True, to, send, recv).wait_send()

        @pl.when(has_down)
        def _():
            for to in range(2):
                rim(buf, b, c, False, to, send, recv).wait_send()

        inside(buf, b, c, send, recv).wait_send()

    def rims_arrive(buf, b, send, recv):
        @pl.when(has_down)
        def _():
            for ch in range(2):
                rim(buf, b, ch, True, 0, send, recv).wait_recv()

        @pl.when(has_up)
        def _():
            for ch in range(2):
                rim(buf, b, ch, False, 0, send, recv).wait_recv()

    def fill_rest(buf, dst, b, send, recv, flip):
        inside(buf, b, other, send, recv).wait_recv()
        for z in range(depth):
            spread(dst, b, z + 1, other, buf[b, z + 1, other], flip)
        rims_arrive(buf, b, send, recv)
        for q in (0, depth + 1):
            for ch in range(2):
                spread(dst, b, q, ch, buf[b, q, ch], flip)

    def conv(src, weight, b, z):
        wide = dot(weight[...], src[b, 3 * z:3 * z + 9].reshape(18 * half, PLANE))
        above = pltpu.roll(wide[:half], WY, 1)
        below = pltpu.roll(wide[2 * half:], PLANE - WY, 1)
        return wide[half:2 * half] + jnp.where(has_above, above, 0.0) + jnp.where(has_below, below, 0.0)

    rim_zero(x)
    rim_zero(g)
    for b in range(batches):
        mask = live[b].astype(BF16)
        for z in range(depth):
            x[b, z + 1, c] = act[b, :, z * PLANE:(z + 1) * PLANE] * mask

    pl.semaphore_wait(barrier, count + has_up.astype(jnp.int32) + has_down.astype(jnp.int32))
    for b in range(batches):
        send_all(x, b, xs, xr)

    for d in range(3):
        wf[d * half:(d + 1) * half] = jnp.concatenate(
            [w[9 * a + 3 * d + e, c] for a in range(3) for e in range(3)], axis=1
        )
    pick_own = (
        lax.broadcasted_iota(jnp.int32, (half, 2 * half), 1)
        == lax.broadcasted_iota(jnp.int32, (half, 2 * half), 0) + c * half
    )
    turned = dot_nt(
        jnp.where(pick_own, 1.0, 0.0).astype(BF16), w[...].reshape(54 * half, 2 * half)
    ).astype(BF16)
    for d in range(3):
        wb[d * half:(d + 1) * half] = jnp.concatenate(
            [
                turned[:, (9 * (2 - a) + 3 * (2 - d)) * 2 * half:(9 * (2 - a) + 3 * (2 - d) + 3) * 2 * half]
                for a in range(3)
            ],
            axis=1,
        )
    for b in range(batches):
        for z in range(depth):
            spread(xe, b, z + 1, c, x[b, z + 1, c], False)

    for b in range(batches):
        fill_rest(x, xe, b, xs, xr, False)
        for z in range(depth):
            pre = conv(xe, wf, b, z)
            s = 1.0 / (1.0 + jnp.exp(-pre))
            span = slice(z * PLANE, (z + 1) * PLANE)
            out[b, :, span] = (live[b] * (x[b, z + 1, c].astype(F32) + pre * s)).astype(BF16)
            slope = s * (1.0 + pre * (1.0 - s))
            own = (cot[b, :, span].astype(F32) * live[b] * slope).astype(BF16)
            g[b, z + 1, c] = own
        send_all(g, b, gs, gr)
        for z in range(depth):
            own = g[b, z + 1, c]
            spread(ge, b, z + 1, c, own, True)
            own = own.astype(F32)
            gd[b, z, 0] = jnp.where(has_below, pltpu.roll(own, PLANE - WY, 1), 0.0).astype(BF16)
            gd[b, z, 1] = g[b, z + 1, c]
            gd[b, z, 2] = jnp.where(has_above, pltpu.roll(own, WY, 1), 0.0).astype(BF16)

    per = part.shape[1] // ROWS
    for i in range(TILES, per * count):
        part[i // per, (i % per) * ROWS:(i % per + 1) * ROWS] = jnp.zeros((ROWS, 128), F32)
    for a in range(3):
        acc = None
        for b in range(batches):
            for z in range(depth):
                q = z + a
                one = dot_nt(
                    gd[b, z].reshape(3 * half, PLANE),
                    xe[b, 3 * q:3 * q + 3].reshape(6 * half, PLANE),
                )
                acc = one if acc is None else acc + one
        body = acc[:, :4 * half]
        rest = acc[:, 4 * half:]
        mid = 3 * half // 2
        body = jnp.concatenate(
            [body, jnp.concatenate([rest[:mid], rest[mid:]], axis=1)], axis=0
        )
        for h in range(9):
            i = 9 * a + h
            part[i // per, (i % per) * ROWS:(i % per + 1) * ROWS] = body[h * ROWS:(h + 1) * ROWS]

    def scatter(j):
        r, device = member(j)
        return pltpu.make_async_remote_copy(
            src_ref=part.at[r], dst_ref=landed.at[rank], send_sem=rs.at[r], recv_sem=rr.at[rank],
            device_id=device, device_id_type=MESH,
        )

    def scattered(j):
        r, device = member(j)
        return pltpu.make_async_remote_copy(
            src_ref=part.at[r], dst_ref=landed.at[r], send_sem=rs.at[r], recv_sem=rr.at[r],
            device_id=device, device_id_type=MESH,
        )

    def gather(j):
        r, device = member(j)
        return pltpu.make_async_remote_copy(
            src_ref=total.at[rank], dst_ref=total.at[rank], send_sem=ts.at[r], recv_sem=tr.at[rank],
            device_id=device, device_id_type=MESH,
        )

    def gathered(j):
        r, device = member(j)
        return pltpu.make_async_remote_copy(
            src_ref=total.at[r], dst_ref=total.at[r], send_sem=ts.at[r], recv_sem=tr.at[r],
            device_id=device, device_id_type=MESH,
        )

    @pl.loop(1, count)
    def _(j):
        scatter(j).start()

    landed[rank] = part[rank]

    def backward(b):
        fill_rest(g, ge, b, gs, gr, True)
        for z in range(depth):
            back = conv(ge, wb, b, z)
            span = slice(z * PLANE, (z + 1) * PLANE)
            grad_in[b, :, span] = (live[b] * (cot[b, :, span].astype(F32) + back)).astype(BF16)

    backward(0)

    @pl.loop(1, count)
    def _(j):
        scattered(j).wait_recv()

    summed = landed[0]
    for i in range(1, count):
        summed = summed + landed[i]
    total[rank] = (summed * scale).astype(BF16)

    @pl.loop(1, count)
    def _(j):
        gather(j).start()

    for b in range(1, batches):
        backward(b)

    for b in range(batches):
        sent_all(x, b, xs, xr)
        sent_all(g, b, gs, gr)

    @pl.loop(1, count)
    def _(j):
        scatter(j).wait_send()
        gather(j).wait_send()
        gathered(j).wait_recv()

    def tile(i):
        return total[i // per, (i % per) * ROWS:(i % per + 1) * ROWS].astype(F32)

    for a in range(3):
        for h in range(6):
            d, low = h // 2, (h % 2) * ROWS
            two = tile(9 * a + h)
            one = tile(9 * a + 6 + h % 3)
            k = 9 * a + 3 * d
            wg[k, low:low + ROWS] = two[:, :2 * half]
            wg[k + 1, low:low + ROWS] = two[:, 2 * half:]
            wg[k + 2, low:low + ROWS] = one[:, (h // 3) * 2 * half:(h // 3 + 1) * 2 * half]


def shards(tiles, dps, activations, occupancy, weight, cotangent):
    batches, half, depth, plane = activations.shape
    inner = depth * plane
    count = tiles * dps
    per = -(-TILES // count)
    scale = 1.0 / math.sqrt(batches * dps * depth * tiles * plane)
    act = activations.reshape(batches, half, inner)
    cot = cotangent.reshape(batches, half, inner)
    w = weight.reshape(27, 2, half, 2 * half)
    vmem = pl.BlockSpec(memory_space=pltpu.VMEM)
    out, grad_in, wg = pl.pallas_call(
        functools.partial(kernel, tiles, dps, scale),
        out_shape=(
            jax.ShapeDtypeStruct((batches, half, inner), BF16),
            jax.ShapeDtypeStruct((batches, half, inner), BF16),
            jax.ShapeDtypeStruct((27, half, 2 * half), F32),
        ),
        in_specs=[vmem, vmem, pl.BlockSpec(memory_space=pltpu.SMEM), vmem],
        out_specs=(vmem, vmem, vmem),
        scratch_shapes=[
            pltpu.VMEM((batches, depth + 2, 2, half, plane), BF16),
            pltpu.VMEM((batches, 3 * (depth + 2), 2, half, plane), BF16),
            pltpu.VMEM((batches, depth + 2, 2, half, plane), BF16),
            pltpu.VMEM((batches, 3 * (depth + 2), 2, half, plane), BF16),
            pltpu.VMEM((batches, depth, 3, half, plane), BF16),
            pltpu.VMEM((3 * half, 18 * half), BF16),
            pltpu.VMEM((3 * half, 18 * half), BF16),
            pltpu.VMEM((count, per * ROWS, 128), F32),
            pltpu.VMEM((count, per * ROWS, 128), F32),
            pltpu.VMEM((count, per * ROWS, 128), BF16),
            pltpu.SemaphoreType.DMA((batches, 5)),
            pltpu.SemaphoreType.DMA((batches, 5)),
            pltpu.SemaphoreType.DMA((batches, 5)),
            pltpu.SemaphoreType.DMA((batches, 5)),
            pltpu.SemaphoreType.DMA((count,)),
            pltpu.SemaphoreType.DMA((count,)),
            pltpu.SemaphoreType.DMA((count,)),
            pltpu.SemaphoreType.DMA((count,)),
        ],
        compiler_params=pltpu.CompilerParams(
            collective_id=0, has_side_effects=True, vmem_limit_bytes=40 * 1024 * 1024
        ),
        cost_estimate=pl.CostEstimate(flops=1400000000, bytes_accessed=2000000, transcendentals=131072),
    )(act, cot, occupancy, w)
    shape = (batches, half, depth, plane)
    return out.reshape(shape), grad_in.reshape(shape), wg


def solution(mesh):
    tiles, dps = mesh.shape["tile"], mesh.shape["dp"]
    return jax.shard_map(
        functools.partial(shards, tiles, dps),
        mesh=mesh,
        in_specs=(
            P(("groups", "dp"), "chan", "tile", None),
            P(("groups", "dp"), "tile", None, None),
            P(),
            P(("groups", "dp"), "chan", "tile", None),
        ),
        out_specs=(
            P(("groups", "dp"), "chan", "tile", None),
            P(("groups", "dp"), "chan", "tile", None),
            P("groups", "chan", None),
        ),
        check_vma=False,
    )
```

```python
import functools
import math

import jax
import jax.numpy as jnp
from jax import lax
from jax.experimental import pallas as pl
from jax.experimental.pallas import tpu as pltpu
from jax.sharding import PartitionSpec as P

E = 8
GX = 2
GY = 2
WY = GY * E
PLANE = GX * E * WY
MESH = pl.DeviceIdType.MESH
BF16 = jnp.bfloat16
F32 = jnp.float32
ROWS = 16
REACH = 32000.0
TINY = 1e-30


def dot(a, b):
    return lax.dot_general(a, b, (((1,), (0,)), ((), ())), preferred_element_type=F32)


def dot_nt(a, b):
    return lax.dot_general(a, b, (((1,), (1,)), ((), ())), preferred_element_type=F32)


def grades(value):
    top = jnp.max(jnp.abs(value), axis=0, keepdims=True)
    return jnp.ceil(jnp.log2(jnp.maximum(top, TINY)))


def code(value, grade, data):
    whole = jnp.round(value * (jnp.exp2(-grade) * REACH)).astype(jnp.int32)
    rows = lax.broadcasted_iota(jnp.int32, value.shape, 0)
    return jnp.where(rows == data, grade.astype(jnp.int32), whole).astype(jnp.int16)


def decode(coded, data):
    wide = coded.astype(jnp.int32).astype(F32)
    rows = lax.broadcasted_iota(jnp.int32, wide.shape, 0)
    grade = jnp.max(jnp.where(rows == data, wide, -REACH), axis=0, keepdims=True)
    return jnp.where(rows < data, wide, 0.0) * (jnp.exp2(grade) * (1.0 / REACH))


def lanes(rows):
    return lax.broadcasted_iota(jnp.int32, (rows, PLANE), 1)


def kernel(
    tiles, dps, scale, data,
    act_far, cot_far, occ, w_far, out_far, grad_far, wg_far,
    act, cot, w, out, grad_in, wg, cots, outs, x, xe, g, ge, gd, wf, wb, flat, part, landed, total,
    near, xs, xr, gs, gr, rs, rr, ts, tr,
):
    batches, half, depth, _ = act.shape
    fetch_act = pltpu.make_async_copy(act_far, act, near.at[0])
    fetch_w = pltpu.make_async_copy(w_far, w, near.at[1])
    fetch_cot = pltpu.make_async_copy(cot_far, cot, near.at[2])
    fetch_act.start()
    fetch_w.start()
    fetch_cot.start()
    me = {name: lax.axis_index(name) for name in ("tile", "dp", "chan")}
    t, c = me["tile"], me["chan"]
    other = 1 - c
    count = tiles * dps
    rank = t * dps + me["dp"]
    has_up = t < tiles - 1
    has_down = t > 0

    def member(j):
        r = lax.rem(rank + j, count)
        return r, {"tile": r // dps, "dp": lax.rem(r, dps)}

    barrier = pltpu.get_barrier_semaphore()

    def greet(device):
        pl.semaphore_signal(barrier, inc=1, device_id=device, device_id_type=MESH)

    greet({"chan": other})

    @pl.when(has_up)
    def _():
        greet({"tile": t + 1, "chan": other})

    @pl.when(has_down)
    def _():
        greet({"tile": t - 1, "chan": other})

    @pl.loop(1, count)
    def _(j):
        greet(member(j)[1])

    place = lanes(half)
    row = place // WY
    col = place % WY
    from_left = jnp.where(col > 0, 1.0, 0.0).astype(BF16)
    from_right = jnp.where(col < WY - 1, 1.0, 0.0).astype(BF16)
    has_above = row > 0
    has_below = row < GX * E - 1

    def live_of(b):
        def pick(i):
            return jnp.where(col < E, occ[b, 0, i, 0], occ[b, 0, i, 1])
        return jnp.where(row < E, pick(0), pick(1)).astype(F32)

    live = [live_of(b) for b in range(batches)]

    def spread(dst, b, q, ch, value, flip):
        first, last = (2, 0) if flip else (0, 2)
        dst[b, 3 * q + first, ch] = pltpu.roll(value, 1, 1) * from_left
        dst[b, 3 * q + 1, ch] = value
        dst[b, 3 * q + last, ch] = pltpu.roll(value, PLANE - 1, 1) * from_right

    def rim_zero(buf):
        zeros = jnp.zeros((half, PLANE), BF16)

        @pl.when(jnp.logical_not(has_down))
        def _():
            for b in range(batches):
                for ch in range(2):
                    buf[b, 0, ch] = zeros

        @pl.when(jnp.logical_not(has_up))
        def _():
            for b in range(batches):
                for ch in range(2):
                    buf[b, depth + 1, ch] = zeros

    def inside(buf, b, ch, send, recv):
        ref = buf.at[b, pl.ds(1, depth), ch]
        return pltpu.make_async_remote_copy(
            src_ref=ref, dst_ref=ref, send_sem=send.at[b, 0], recv_sem=recv.at[b, 0],
            device_id={"chan": other}, device_id_type=MESH,
        )

    def rim(buf, b, ch, up, to, send, recv):
        side = 1 if up else 3
        return pltpu.make_async_remote_copy(
            src_ref=buf.at[b, depth if up else 1, ch],
            dst_ref=buf.at[b, 0 if up else depth + 1, ch],
            send_sem=send.at[b, side + to], recv_sem=recv.at[b, side + ch],
            device_id={"tile": t + 1 if up else t - 1, "chan": to}, device_id_type=MESH,
        )

    def send_all(buf, b, send, recv):
        @pl.when(has_up)
        def _():
            for to in range(2):
                rim(buf, b, c, True, to, send, recv).start()

        @pl.when(has_down)
        def _():
            for to in range(2):
                rim(buf, b, c, False, to, send, recv).start()

        inside(buf, b, c, send, recv).start()

    def sent_all(buf, b, send, recv):
        @pl.when(has_up)
        def _():
            for to in range(2):
                rim(buf, b, c, True, to, send, recv).wait_send()

        @pl.when(has_down)
        def _():
            for to in range(2):
                rim(buf, b, c, False, to, send, recv).wait_send()

        inside(buf, b, c, send, recv).wait_send()

    def rims_arrive(buf, b, send, recv):
        @pl.when(has_down)
        def _():
            for ch in range(2):
                rim(buf, b, ch, True, 0, send, recv).wait_recv()

        @pl.when(has_up)
        def _():
            for ch in range(2):
                rim(buf, b, ch, False, 0, send, recv).wait_recv()

    def fill_rest(buf, dst, b, send, recv, flip):
        inside(buf, b, other, send, recv).wait_recv()
        for z in range(depth):
            spread(dst, b, z + 1, other, buf[b, z + 1, other], flip)
        rims_arrive(buf, b, send, recv)
        for q in (0, depth + 1):
            for ch in range(2):
                spread(dst, b, q, ch, buf[b, q, ch], flip)

    def conv(src, weight, b, z):
        wide = dot(weight[...], src[b, 3 * z:3 * z + 9].reshape(18 * half, PLANE))
        above = pltpu.roll(wide[:half], WY, 1)
        below = pltpu.roll(wide[2 * half:], PLANE - WY, 1)
        return wide[half:2 * half] + jnp.where(has_above, above, 0.0) + jnp.where(has_below, below, 0.0)

    rim_zero(x)
    rim_zero(g)
    fetch_act.wait()
    for b in range(batches):
        planes = jnp.swapaxes(act[b].astype(F32), 0, 1)
        for z in range(depth):
            x[b, z + 1, c] = (planes[z] * live[b]).astype(BF16)

    pl.semaphore_wait(barrier, count + has_up.astype(jnp.int32) + has_down.astype(jnp.int32))
    for b in range(batches):
        send_all(x, b, xs, xr)

    fetch_w.wait()
    for d in range(3):
        wf[d * half:(d + 1) * half] = jnp.concatenate(
            [w[9 * a + 3 * d + e, c] for a in range(3) for e in range(3)], axis=1
        )
    pick_own = (
        lax.broadcasted_iota(jnp.int32, (half, 2 * half), 1)
        == lax.broadcasted_iota(jnp.int32, (half, 2 * half), 0) + c * half
    )
    turned = dot_nt(
        jnp.where(pick_own, 1.0, 0.0).astype(BF16), w[...].reshape(54 * half, 2 * half)
    ).astype(BF16)
    for d in range(3):
        wb[d * half:(d + 1) * half] = jnp.concatenate(
            [
                turned[:, (9 * (2 - a) + 3 * (2 - d)) * 2 * half:(9 * (2 - a) + 3 * (2 - d) + 3) * 2 * half]
                for a in range(3)
            ],
            axis=1,
        )
    for b in range(batches):
        for z in range(depth):
            spread(xe, b, z + 1, c, x[b, z + 1, c], False)
    fetch_cot.wait()
    for b in range(batches):
        cots[b] = jnp.swapaxes(cot[b].astype(F32), 0, 1)

    for b in range(batches):
        fill_rest(x, xe, b, xs, xr, False)
        for z in range(depth):
            pre = conv(xe, wf, b, z)
            s = 1.0 / (1.0 + jnp.exp(-pre))
            outs[b, z] = live[b] * (x[b, z + 1, c].astype(F32) + pre * s)
            slope = s * (1.0 + pre * (1.0 - s))
            own = (cots[b, z] * live[b] * slope).astype(BF16)
            g[b, z + 1, c] = own
        if b == 0:
            send_all(g, b, gs, gr)
        for z in range(depth):
            own = g[b, z + 1, c].astype(F32)
            gd[b, z, 0] = jnp.where(has_below, pltpu.roll(own, PLANE - WY, 1), 0.0).astype(BF16)
            gd[b, z, 1] = g[b, z + 1, c]
            gd[b, z, 2] = jnp.where(has_above, pltpu.roll(own, WY, 1), 0.0).astype(BF16)

    fold = 9 * half // 2
    flat[3 * fold:] = jnp.zeros((flat.shape[0] - 3 * fold, 128), F32)
    for a in range(3):
        acc = None
        for b in range(batches):
            for z in range(depth):
                q = z + a
                one = dot_nt(
                    gd[b, z].reshape(3 * half, PLANE),
                    xe[b, 3 * q:3 * q + 3].reshape(6 * half, PLANE),
                )
                acc = one if acc is None else acc + one
        body = acc[:, :4 * half]
        rest = acc[:, 4 * half:]
        mid = 3 * half // 2
        flat[a * fold:a * fold + 3 * half] = body
        flat[a * fold + 3 * half:(a + 1) * fold] = jnp.concatenate([rest[:mid], rest[mid:]], axis=1)
    rows = part.shape[1]
    grade = grades(flat[:3 * fold])
    for i in range(count):
        part[i] = code(flat[i * data:i * data + rows], grade, data)

    def scatter(j):
        r, device = member(j)
        return pltpu.make_async_remote_copy(
            src_ref=part.at[r], dst_ref=landed.at[rank], send_sem=rs.at[r], recv_sem=rr.at[rank],
            device_id=device, device_id_type=MESH,
        )

    def scattered(j):
        r, device = member(j)
        return pltpu.make_async_remote_copy(
            src_ref=part.at[r], dst_ref=landed.at[r], send_sem=rs.at[r], recv_sem=rr.at[r],
            device_id=device, device_id_type=MESH,
        )

    def gather(j):
        r, device = member(j)
        return pltpu.make_async_remote_copy(
            src_ref=total.at[rank], dst_ref=total.at[rank], send_sem=ts.at[r], recv_sem=tr.at[rank],
            device_id=device, device_id_type=MESH,
        )

    def gathered(j):
        r, device = member(j)
        return pltpu.make_async_remote_copy(
            src_ref=total.at[r], dst_ref=total.at[r], send_sem=ts.at[r], recv_sem=tr.at[r],
            device_id=device, device_id_type=MESH,
        )

    @pl.loop(1, count)
    def _(j):
        scatter(j).start()

    landed[rank] = part[rank]
    for b in range(1, batches):
        send_all(g, b, gs, gr)
    for b in range(batches):
        for z in range(depth):
            spread(ge, b, z + 1, c, g[b, z + 1, c], True)
        out[b] = jnp.swapaxes(outs[b], 0, 1).astype(BF16)
    leave_out = pltpu.make_async_copy(out, out_far, near.at[3])
    leave_out.start()

    def backward(b):
        fill_rest(g, ge, b, gs, gr, True)
        for z in range(depth):
            back = conv(ge, wb, b, z)
            outs[b, z] = live[b] * (cots[b, z] + back)
        grad_in[b] = jnp.swapaxes(outs[b], 0, 1).astype(BF16)

    backward(0)

    @pl.loop(1, count)
    def _(j):
        scattered(j).wait_recv()

    summed = decode(landed[0], data)
    for i in range(1, count):
        summed = summed + decode(landed[i], data)
    total[rank] = code(summed, grades(summed), data)

    @pl.loop(1, count)
    def _(j):
        gather(j).start()

    for b in range(1, batches):
        backward(b)
    leave_grad = pltpu.make_async_copy(grad_in, grad_far, near.at[4])
    leave_grad.start()

    for b in range(batches):
        sent_all(x, b, xs, xr)
        sent_all(g, b, gs, gr)

    @pl.loop(1, count)
    def _(j):
        scatter(j).wait_send()
        gather(j).wait_send()
        gathered(j).wait_recv()

    for i in range(count):
        flat[i * data:(i + 1) * data] = decode(total[i], data)[:data] * scale

    for a in range(3):
        for h in range(6):
            d, low = h // 2, (h % 2) * ROWS
            start = a * fold + h * ROWS
            two = flat[start:start + ROWS]
            start = a * fold + 3 * half + (h % 3) * ROWS
            one = flat[start:start + ROWS]
            k = 9 * a + 3 * d
            wg[k, low:low + ROWS] = two[:, :2 * half]
            wg[k + 1, low:low + ROWS] = two[:, 2 * half:]
            wg[k + 2, low:low + ROWS] = one[:, (h // 3) * 2 * half:(h // 3 + 1) * 2 * half]
    leave_wg = pltpu.make_async_copy(wg, wg_far, near.at[5])
    leave_wg.start()
    leave_out.wait()
    leave_grad.wait()
    leave_wg.wait()


def finish(a, b, c, a_out, b_out, c_out, a_mid, b_mid, c_mid, sems):
    loads, stores = [], []
    for i, (src, mid, dst) in enumerate(((a, a_mid, a_out), (b, b_mid, b_out), (c, c_mid, c_out))):
        loads.append(pltpu.make_async_copy(src, mid, sems.at[0, i]))
        stores.append(pltpu.make_async_copy(mid, dst, sems.at[1, i]))
    for load in loads:
        load.start()
    for load, store in zip(loads, stores):
        load.wait()
        store.start()
    for store in stores:
        store.wait()


def shards(tiles, dps, activations, occupancy, weight, cotangent):
    batches, half, depth, plane = activations.shape
    count = tiles * dps
    folded = 27 * half * 2 * half // 128
    data = -(-folded // count)
    rows = -(-(data + 1) // ROWS) * ROWS
    scale = 1.0 / math.sqrt(batches * dps * depth * tiles * plane)
    w = weight.reshape(27, 2, half, 2 * half)
    vmem = pl.BlockSpec(memory_space=pltpu.VMEM)
    far = pl.BlockSpec(memory_space=pltpu.HBM)
    full = (batches, half, depth, plane)
    results = pl.pallas_call(
        functools.partial(kernel, tiles, dps, scale, data),
        out_shape=(
            jax.ShapeDtypeStruct(full, BF16),
            jax.ShapeDtypeStruct(full, BF16),
            jax.ShapeDtypeStruct((27, half, 2 * half), F32),
        ),
        in_specs=[far, far, pl.BlockSpec(memory_space=pltpu.SMEM), far],
        out_specs=(far, far, far),
        scratch_shapes=[
            pltpu.VMEM(full, BF16),
            pltpu.VMEM(full, BF16),
            pltpu.VMEM(w.shape, BF16),
            pltpu.VMEM(full, BF16),
            pltpu.VMEM(full, BF16),
            pltpu.VMEM((27, half, 2 * half), F32),
            pltpu.VMEM((batches, depth, half, plane), F32),
            pltpu.VMEM((batches, depth, half, plane), F32),
            pltpu.VMEM((batches, depth + 2, 2, half, plane), BF16),
            pltpu.VMEM((batches, 3 * (depth + 2), 2, half, plane), BF16),
            pltpu.VMEM((batches, depth + 2, 2, half, plane), BF16),
            pltpu.VMEM((batches, 3 * (depth + 2), 2, half, plane), BF16),
            pltpu.VMEM((batches, depth, 3, half, plane), BF16),
            pltpu.VMEM((3 * half, 18 * half), BF16),
            pltpu.VMEM((3 * half, 18 * half), BF16),
            pltpu.VMEM(((count - 1) * data + rows, 128), F32),
            pltpu.VMEM((count, rows, 128), jnp.int16),
            pltpu.VMEM((count, rows, 128), jnp.int16),
            pltpu.VMEM((count, rows, 128), jnp.int16),
            pltpu.SemaphoreType.DMA((6,)),
            pltpu.SemaphoreType.DMA((batches, 5)),
            pltpu.SemaphoreType.DMA((batches, 5)),
            pltpu.SemaphoreType.DMA((batches, 5)),
            pltpu.SemaphoreType.DMA((batches, 5)),
            pltpu.SemaphoreType.DMA((count,)),
            pltpu.SemaphoreType.DMA((count,)),
            pltpu.SemaphoreType.DMA((count,)),
            pltpu.SemaphoreType.DMA((count,)),
        ],
        compiler_params=pltpu.CompilerParams(
            collective_id=0, has_side_effects=True, vmem_limit_bytes=60 * 1024 * 1024
        ),
        cost_estimate=pl.CostEstimate(flops=1400000000, bytes_accessed=2000000, transcendentals=131072),
    )(activations, cotangent, occupancy, w)
    return pl.pallas_call(
        finish,
        out_shape=tuple(jax.ShapeDtypeStruct(r.shape, r.dtype) for r in results),
        in_specs=[far, far, far],
        out_specs=(far, far, far),
        scratch_shapes=[pltpu.VMEM(r.shape, r.dtype) for r in results] + [pltpu.SemaphoreType.DMA((2, 3))],
        compiler_params=pltpu.CompilerParams(vmem_limit_bytes=60 * 1024 * 1024),
    )(*results)


def solution(mesh):
    tiles, dps = mesh.shape["tile"], mesh.shape["dp"]
    return jax.shard_map(
        functools.partial(shards, tiles, dps),
        mesh=mesh,
        in_specs=(
            P(("groups", "dp"), "chan", "tile", None),
            P(("groups", "dp"), "tile", None, None),
            P(),
            P(("groups", "dp"), "chan", "tile", None),
        ),
        out_specs=(
            P(("groups", "dp"), "chan", "tile", None),
            P(("groups", "dp"), "chan", "tile", None),
            P("groups", "chan", None),
        ),
        check_vma=False,
    )
```

```python
import functools
import math

import jax
import jax.numpy as jnp
from jax import lax
from jax.experimental import pallas as pl
from jax.experimental.pallas import tpu as pltpu
from jax.sharding import PartitionSpec as P

E = 8
GX = 2
GY = 2
WY = GY * E
PLANE = GX * E * WY
MESH = pl.DeviceIdType.MESH
BF16 = jnp.bfloat16
F32 = jnp.float32
ROWS = 16
REACH = 32000.0
TINY = 1e-30


def dot(a, b):
    return lax.dot_general(a, b, (((1,), (0,)), ((), ())), preferred_element_type=F32)


def dot_nt(a, b):
    return lax.dot_general(a, b, (((1,), (1,)), ((), ())), preferred_element_type=F32)


def grades(value):
    top = jnp.max(jnp.abs(value), axis=0, keepdims=True)
    return jnp.ceil(jnp.log2(jnp.maximum(top, TINY)))


def code(value, grade, data):
    whole = jnp.round(value * (jnp.exp2(-grade) * REACH)).astype(jnp.int32)
    rows = lax.broadcasted_iota(jnp.int32, value.shape, 0)
    return jnp.where(rows == data, grade.astype(jnp.int32), whole).astype(jnp.int16)


def decode(coded, data):
    wide = coded.astype(jnp.int32).astype(F32)
    rows = lax.broadcasted_iota(jnp.int32, wide.shape, 0)
    grade = jnp.max(jnp.where(rows == data, wide, -REACH), axis=0, keepdims=True)
    return jnp.where(rows < data, wide, 0.0) * (jnp.exp2(grade) * (1.0 / REACH))


def lanes(rows):
    return lax.broadcasted_iota(jnp.int32, (rows, PLANE), 1)


def kernel(
    tiles, dps, data,
    act_far, cot_far, occ, w_far, out_far, grad_far, total_far,
    act, cot, w, out, grad_in, cots, outs, x, xe, g, ge, gd, wf, wb, flat, part, landed, total,
    near, xs, xr, gs, gr, rs, rr, ts, tr,
):
    batches, half, depth, _ = act.shape
    fetch_act = pltpu.make_async_copy(act_far, act, near.at[0])
    fetch_w = pltpu.make_async_copy(w_far, w, near.at[1])
    fetch_cot = pltpu.make_async_copy(cot_far, cot, near.at[2])
    fetch_act.start()
    fetch_w.start()
    fetch_cot.start()
    me = {name: lax.axis_index(name) for name in ("tile", "dp", "chan")}
    t, c = me["tile"], me["chan"]
    other = 1 - c
    count = tiles * dps
    rank = t * dps + me["dp"]
    has_up = t < tiles - 1
    has_down = t > 0

    def member(j):
        r = lax.rem(rank + j, count)
        return r, {"tile": r // dps, "dp": lax.rem(r, dps)}

    barrier = pltpu.get_barrier_semaphore()

    def greet(device):
        pl.semaphore_signal(barrier, inc=1, device_id=device, device_id_type=MESH)

    greet({"chan": other})

    @pl.when(has_up)
    def _():
        greet({"tile": t + 1, "chan": other})

    @pl.when(has_down)
    def _():
        greet({"tile": t - 1, "chan": other})

    @pl.loop(1, count)
    def _(j):
        greet(member(j)[1])

    place = lanes(half)
    row = place // WY
    col = place % WY
    from_left = jnp.where(col > 0, 1.0, 0.0).astype(BF16)
    from_right = jnp.where(col < WY - 1, 1.0, 0.0).astype(BF16)
    has_above = row > 0
    has_below = row < GX * E - 1

    def live_of(b):
        def pick(i):
            return jnp.where(col < E, occ[b, 0, i, 0], occ[b, 0, i, 1])
        return jnp.where(row < E, pick(0), pick(1)).astype(F32)

    live = [live_of(b) for b in range(batches)]

    def spread(dst, b, q, ch, value, flip):
        first, last = (2, 0) if flip else (0, 2)
        dst[b, 3 * q + first, ch] = pltpu.roll(value, 1, 1) * from_left
        dst[b, 3 * q + 1, ch] = value
        dst[b, 3 * q + last, ch] = pltpu.roll(value, PLANE - 1, 1) * from_right

    def rim_zero(buf):
        zeros = jnp.zeros((half, PLANE), BF16)

        @pl.when(jnp.logical_not(has_down))
        def _():
            for b in range(batches):
                for ch in range(2):
                    buf[b, 0, ch] = zeros

        @pl.when(jnp.logical_not(has_up))
        def _():
            for b in range(batches):
                for ch in range(2):
                    buf[b, depth + 1, ch] = zeros

    def inside(buf, b, ch, send, recv):
        ref = buf.at[b, pl.ds(1, depth), ch]
        return pltpu.make_async_remote_copy(
            src_ref=ref, dst_ref=ref, send_sem=send.at[b, 0], recv_sem=recv.at[b, 0],
            device_id={"chan": other}, device_id_type=MESH,
        )

    def rim(buf, b, ch, up, to, send, recv):
        side = 1 if up else 3
        return pltpu.make_async_remote_copy(
            src_ref=buf.at[b, depth if up else 1, ch],
            dst_ref=buf.at[b, 0 if up else depth + 1, ch],
            send_sem=send.at[b, side + to], recv_sem=recv.at[b, side + ch],
            device_id={"tile": t + 1 if up else t - 1, "chan": to}, device_id_type=MESH,
        )

    def send_all(buf, b, send, recv):
        @pl.when(has_up)
        def _():
            for to in range(2):
                rim(buf, b, c, True, to, send, recv).start()

        @pl.when(has_down)
        def _():
            for to in range(2):
                rim(buf, b, c, False, to, send, recv).start()

        inside(buf, b, c, send, recv).start()

    def sent_all(buf, b, send, recv):
        @pl.when(has_up)
        def _():
            for to in range(2):
                rim(buf, b, c, True, to, send, recv).wait_send()

        @pl.when(has_down)
        def _():
            for to in range(2):
                rim(buf, b, c, False, to, send, recv).wait_send()

        inside(buf, b, c, send, recv).wait_send()

    def rims_arrive(buf, b, send, recv):
        @pl.when(has_down)
        def _():
            for ch in range(2):
                rim(buf, b, ch, True, 0, send, recv).wait_recv()

        @pl.when(has_up)
        def _():
            for ch in range(2):
                rim(buf, b, ch, False, 0, send, recv).wait_recv()

    def fill_inner(buf, dst, b, send, recv, flip):
        inside(buf, b, other, send, recv).wait_recv()
        for z in range(depth):
            spread(dst, b, z + 1, other, buf[b, z + 1, other], flip)

    def fill_rims(buf, dst, b, send, recv, flip):
        rims_arrive(buf, b, send, recv)
        for q in (0, depth + 1):
            for ch in range(2):
                spread(dst, b, q, ch, buf[b, q, ch], flip)

    def conv(src, weight, b, z):
        wide = dot(weight[...], src[b, 3 * z:3 * z + 9].reshape(18 * half, PLANE))
        above = pltpu.roll(wide[:half], WY, 1)
        below = pltpu.roll(wide[2 * half:], PLANE - WY, 1)
        return wide[half:2 * half] + jnp.where(has_above, above, 0.0) + jnp.where(has_below, below, 0.0)

    rim_zero(x)
    rim_zero(g)
    fetch_act.wait()
    for b in range(batches):
        planes = jnp.swapaxes(act[b].astype(F32), 0, 1)
        for z in range(depth):
            x[b, z + 1, c] = (planes[z] * live[b]).astype(BF16)

    pl.semaphore_wait(barrier, count + has_up.astype(jnp.int32) + has_down.astype(jnp.int32))
    for b in range(batches):
        send_all(x, b, xs, xr)

    fetch_w.wait()
    for d in range(3):
        wf[d * half:(d + 1) * half] = jnp.concatenate(
            [w[9 * a + 3 * d + e, c] for a in range(3) for e in range(3)], axis=1
        )
    pick_own = (
        lax.broadcasted_iota(jnp.int32, (half, 2 * half), 1)
        == lax.broadcasted_iota(jnp.int32, (half, 2 * half), 0) + c * half
    )
    turned = dot_nt(
        jnp.where(pick_own, 1.0, 0.0).astype(BF16), w[...].reshape(54 * half, 2 * half)
    ).astype(BF16)
    for d in range(3):
        wb[d * half:(d + 1) * half] = jnp.concatenate(
            [
                turned[:, (9 * (2 - a) + 3 * (2 - d)) * 2 * half:(9 * (2 - a) + 3 * (2 - d) + 3) * 2 * half]
                for a in range(3)
            ],
            axis=1,
        )
    for b in range(batches):
        for z in range(depth):
            spread(xe, b, z + 1, c, x[b, z + 1, c], False)
    fetch_cot.wait()
    for b in range(batches):
        cots[b] = jnp.swapaxes(cot[b].astype(F32), 0, 1)

    def forward(b, z):
        pre = conv(xe, wf, b, z)
        s = 1.0 / (1.0 + jnp.exp(-pre))
        outs[b, z] = live[b] * (x[b, z + 1, c].astype(F32) + pre * s)
        slope = s * (1.0 + pre * (1.0 - s))
        own = (cots[b, z] * live[b] * slope).astype(BF16)
        g[b, z + 1, c] = own
        wide = own.astype(F32)
        gd[b, z, 0] = jnp.where(has_below, pltpu.roll(wide, PLANE - WY, 1), 0.0).astype(BF16)
        gd[b, z, 1] = own
        gd[b, z, 2] = jnp.where(has_above, pltpu.roll(wide, WY, 1), 0.0).astype(BF16)

    for b in range(batches):
        fill_inner(x, xe, b, xs, xr, False)
        for z in range(1, depth - 1):
            forward(b, z)
    for b in range(batches):
        fill_rims(x, xe, b, xs, xr, False)
        for z in (0, depth - 1):
            forward(b, z)
        if b == 0:
            send_all(g, b, gs, gr)

    fold = 9 * half // 2
    flat[3 * fold:] = jnp.zeros((flat.shape[0] - 3 * fold, 128), F32)
    for a in range(3):
        acc = None
        for b in range(batches):
            for z in range(depth):
                q = z + a
                one = dot_nt(
                    gd[b, z].reshape(3 * half, PLANE),
                    xe[b, 3 * q:3 * q + 3].reshape(6 * half, PLANE),
                )
                acc = one if acc is None else acc + one
        body = acc[:, :4 * half]
        rest = acc[:, 4 * half:]
        mid = 3 * half // 2
        flat[a * fold:a * fold + 3 * half] = body
        flat[a * fold + 3 * half:(a + 1) * fold] = jnp.concatenate([rest[:mid], rest[mid:]], axis=1)
    rows = part.shape[1]
    grade = grades(flat[:3 * fold])
    for i in range(count):
        part[i] = code(flat[i * data:i * data + rows], grade, data)

    def scatter(j):
        r, device = member(j)
        return pltpu.make_async_remote_copy(
            src_ref=part.at[r], dst_ref=landed.at[rank], send_sem=rs.at[r], recv_sem=rr.at[rank],
            device_id=device, device_id_type=MESH,
        )

    def scattered(j):
        r, device = member(j)
        return pltpu.make_async_remote_copy(
            src_ref=part.at[r], dst_ref=landed.at[r], send_sem=rs.at[r], recv_sem=rr.at[r],
            device_id=device, device_id_type=MESH,
        )

    def gather(j):
        r, device = member(j)
        return pltpu.make_async_remote_copy(
            src_ref=total.at[rank], dst_ref=total.at[rank], send_sem=ts.at[r], recv_sem=tr.at[rank],
            device_id=device, device_id_type=MESH,
        )

    def gathered(j):
        r, device = member(j)
        return pltpu.make_async_remote_copy(
            src_ref=total.at[r], dst_ref=total.at[r], send_sem=ts.at[r], recv_sem=tr.at[r],
            device_id=device, device_id_type=MESH,
        )

    @pl.loop(1, count)
    def _(j):
        scatter(j).start()

    landed[rank] = part[rank]
    for b in range(1, batches):
        send_all(g, b, gs, gr)
    for b in range(batches):
        for z in range(depth):
            spread(ge, b, z + 1, c, g[b, z + 1, c], True)
        out[b] = jnp.swapaxes(outs[b], 0, 1).astype(BF16)
    leave_out = pltpu.make_async_copy(out, out_far, near.at[3])
    leave_out.start()

    def backward(b):
        fill_inner(g, ge, b, gs, gr, True)
        fill_rims(g, ge, b, gs, gr, True)
        for z in range(depth):
            back = conv(ge, wb, b, z)
            outs[b, z] = live[b] * (cots[b, z] + back)
        grad_in[b] = jnp.swapaxes(outs[b], 0, 1).astype(BF16)

    backward(0)

    @pl.loop(1, count)
    def _(j):
        scattered(j).wait_recv()

    summed = decode(landed[0], data)
    for i in range(1, count):
        summed = summed + decode(landed[i], data)
    total[rank] = code(summed, grades(summed), data)

    @pl.loop(1, count)
    def _(j):
        gather(j).start()

    for b in range(1, batches):
        backward(b)
    leave_grad = pltpu.make_async_copy(grad_in, grad_far, near.at[4])
    leave_grad.start()

    @pl.loop(1, count)
    def _(j):
        gathered(j).wait_recv()

    leave_total = pltpu.make_async_copy(total, total_far, near.at[5])
    leave_total.start()
    for b in range(batches):
        sent_all(x, b, xs, xr)
        sent_all(g, b, gs, gr)

    @pl.loop(1, count)
    def _(j):
        scatter(j).wait_send()
        gather(j).wait_send()

    leave_out.wait()
    leave_grad.wait()
    leave_total.wait()


def finish(scale, data, a, b, c, a_out, b_out, wg_out, a_mid, b_mid, total, flat, wg, sems):
    loads = [
        pltpu.make_async_copy(src, mid, sems.at[0, i])
        for i, (src, mid) in enumerate(((c, total), (a, a_mid), (b, b_mid)))
    ]
    stores = [
        pltpu.make_async_copy(mid, dst, sems.at[1, i])
        for i, (mid, dst) in enumerate(((wg, wg_out), (a_mid, a_out), (b_mid, b_out)))
    ]
    for load in loads:
        load.start()
    loads[0].wait()
    count = total.shape[0]
    half = wg.shape[1]
    fold = 9 * half // 2
    for i in range(count):
        flat[i * data:(i + 1) * data] = decode(total[i], data)[:data] * scale

    for a in range(3):
        for h in range(6):
            d, low = h // 2, (h % 2) * ROWS
            start = a * fold + h * ROWS
            two = flat[start:start + ROWS]
            start = a * fold + 3 * half + (h % 3) * ROWS
            one = flat[start:start + ROWS]
            k = 9 * a + 3 * d
            wg[k, low:low + ROWS] = two[:, :2 * half]
            wg[k + 1, low:low + ROWS] = two[:, 2 * half:]
            wg[k + 2, low:low + ROWS] = one[:, (h // 3) * 2 * half:(h // 3 + 1) * 2 * half]
    stores[0].start()
    for load, store in zip(loads[1:], stores[1:]):
        load.wait()
        store.start()
    for store in stores:
        store.wait()


def shards(tiles, dps, activations, occupancy, weight, cotangent):
    batches, half, depth, plane = activations.shape
    count = tiles * dps
    folded = 27 * half * 2 * half // 128
    data = -(-folded // count)
    rows = -(-(data + 1) // ROWS) * ROWS
    scale = 1.0 / math.sqrt(batches * dps * depth * tiles * plane)
    w = weight.reshape(27, 2, half, 2 * half)
    vmem = pl.BlockSpec(memory_space=pltpu.VMEM)
    far = pl.BlockSpec(memory_space=pltpu.HBM)
    full = (batches, half, depth, plane)
    results = pl.pallas_call(
        functools.partial(kernel, tiles, dps, data),
        out_shape=(
            jax.ShapeDtypeStruct(full, BF16),
            jax.ShapeDtypeStruct(full, BF16),
            jax.ShapeDtypeStruct((count, rows, 128), jnp.int16),
        ),
        in_specs=[far, far, pl.BlockSpec(memory_space=pltpu.SMEM), far],
        out_specs=(far, far, far),
        scratch_shapes=[
            pltpu.VMEM(full, BF16),
            pltpu.VMEM(full, BF16),
            pltpu.VMEM(w.shape, BF16),
            pltpu.VMEM(full, BF16),
            pltpu.VMEM(full, BF16),
            pltpu.VMEM((batches, depth, half, plane), F32),
            pltpu.VMEM((batches, depth, half, plane), F32),
            pltpu.VMEM((batches, depth + 2, 2, half, plane), BF16),
            pltpu.VMEM((batches, 3 * (depth + 2), 2, half, plane), BF16),
            pltpu.VMEM((batches, depth + 2, 2, half, plane), BF16),
            pltpu.VMEM((batches, 3 * (depth + 2), 2, half, plane), BF16),
            pltpu.VMEM((batches, depth, 3, half, plane), BF16),
            pltpu.VMEM((3 * half, 18 * half), BF16),
            pltpu.VMEM((3 * half, 18 * half), BF16),
            pltpu.VMEM(((count - 1) * data + rows, 128), F32),
            pltpu.VMEM((count, rows, 128), jnp.int16),
            pltpu.VMEM((count, rows, 128), jnp.int16),
            pltpu.VMEM((count, rows, 128), jnp.int16),
            pltpu.SemaphoreType.DMA((6,)),
            pltpu.SemaphoreType.DMA((batches, 5)),
            pltpu.SemaphoreType.DMA((batches, 5)),
            pltpu.SemaphoreType.DMA((batches, 5)),
            pltpu.SemaphoreType.DMA((batches, 5)),
            pltpu.SemaphoreType.DMA((count,)),
            pltpu.SemaphoreType.DMA((count,)),
            pltpu.SemaphoreType.DMA((count,)),
            pltpu.SemaphoreType.DMA((count,)),
        ],
        compiler_params=pltpu.CompilerParams(
            collective_id=0, has_side_effects=True, vmem_limit_bytes=60 * 1024 * 1024
        ),
        cost_estimate=pl.CostEstimate(flops=1400000000, bytes_accessed=2000000, transcendentals=131072),
    )(activations, cotangent, occupancy, w)
    return pl.pallas_call(
        functools.partial(finish, scale, data),
        out_shape=(
            jax.ShapeDtypeStruct(full, BF16),
            jax.ShapeDtypeStruct(full, BF16),
            jax.ShapeDtypeStruct((27, half, 2 * half), F32),
        ),
        in_specs=[far, far, far],
        out_specs=(far, far, far),
        scratch_shapes=[
            pltpu.VMEM(full, BF16),
            pltpu.VMEM(full, BF16),
            pltpu.VMEM((count, rows, 128), jnp.int16),
            pltpu.VMEM((count * data, 128), F32),
            pltpu.VMEM((27, half, 2 * half), F32),
            pltpu.SemaphoreType.DMA((2, 3)),
        ],
        compiler_params=pltpu.CompilerParams(vmem_limit_bytes=60 * 1024 * 1024),
    )(*results)


def solution(mesh):
    tiles, dps = mesh.shape["tile"], mesh.shape["dp"]
    return jax.shard_map(
        functools.partial(shards, tiles, dps),
        mesh=mesh,
        in_specs=(
            P(("groups", "dp"), "chan", "tile", None),
            P(("groups", "dp"), "tile", None, None),
            P(),
            P(("groups", "dp"), "chan", "tile", None),
        ),
        out_specs=(
            P(("groups", "dp"), "chan", "tile", None),
            P(("groups", "dp"), "chan", "tile", None),
            P("groups", "chan", None),
        ),
        check_vma=False,
    )
```
